512 devices in a mesh: row: 32 (over y, x, core), col: 16 (over z).
Axes of the slice: x: 4, y: 4, z: 16, core: 2. Of those that a mesh axis runs over, the one named last changes fastest.
Arguments:
- nodes: bfloat16 [65536, 128], P(('row', 'col')), may hold values from -6 to 6
- edges: bfloat16 [1572864, 128], P(('row', 'col')), may hold values from -6 to 6
- send_list: int32 [8192, 32], P(('row', 'col')), may hold values from 0 to 127, as said below
- recv_list: int32 [16384, 16], P(('row', 'col')), may hold values from 0 to 127, as said below
- sender_slot: int32 [12288, 128], P(('row', 'col')), may hold values from 0 to 511
- receiver_slot: int32 [12288, 128], P(('row', 'col')), may hold values from 0 to 511
- tile_count: int32 [12288], P(('row', 'col')), may hold values from 0 to 128, as said below
- edge_in_weight: bfloat16 [384, 128], replicated, may hold values from -0.3125 to 0.3125
- edge_out_weight: bfloat16 [2, 128, 128], replicated, may hold values from -0.5 to 0.5
- edge_bias: float32 [3, 128], replicated, may hold values from -3 to 3
- edge_gain: float32 [128], replicated, may hold values from 0.1 to 1.9
- edge_shift: float32 [128], replicated, may hold values from -3 to 3
- node_in_weight: bfloat16 [256, 128], replicated, may hold values from -0.375 to 0.375
- node_out_weight: bfloat16 [2, 128, 128], replicated, may hold values from -0.5 to 0.5
- node_bias: float32 [3, 128], replicated, may hold values from -3 to 3
- node_gain: float32 [128], replicated, may hold values from 0.1 to 1.9
- node_shift: float32 [128], replicated, may hold values from -3 to 3
Outputs:
- new_nodes: bfloat16 [65536, 128], P(('row', 'col'))
- new_edges: bfloat16 [1572864, 128], P(('row', 'col'))
The draws below stay inside these ranges and needn't reach their ends.
Inputs may be any that keep to these rules, and one draw needn't show every extreme that they name: `send_list`: within one row of the list the entries are distinct. `recv_list`: within one row of the list the entries are distinct. `tile_count`: on every device the tiles with count 0 come after all tiles with a nonzero count, and at least one tile has a nonzero count; all tiles before a device's last nonzero one hold 128; some device has all 24 tiles at 128.
All inputs are finite; a program needn't handle non-finite values.
Results may differ from the reference program's by a relative error of at most 0.015.
Values may be sent and summed in bfloat16 or wider, within the bound.
No kernel may reach another device: no remote copies, remote signals or barrier semaphores. Data moves between devices by JAX's collectives and lax.ppermute only.
A program may use at most 64 MiB of HBM per device.

```python
import jax
import jax.numpy as jnp
from jax import lax

LATENT = 128
NODE_DEV = 128
TILES = 24
TILE = 128
SCAP = 32
RCAP = 16
NODES = 65536
EDGES = 1572864
N_ROW = 32
N_COL = 16
DEVICES = 512


def listed_rows(key, rows, width):
    scores = jax.random.randint(key, (rows, NODE_DEV), 0, 1048576) * NODE_DEV + jnp.arange(NODE_DEV, dtype=jnp.int32)[None, :]
    order = jnp.argsort(scores, axis=1, stable=True)
    return order[:, :width].astype(jnp.int32)


def draw_send_list(key, part):
    key = jax.random.fold_in(key, 11)
    return listed_rows(key, N_ROW * N_COL * N_COL, SCAP)


def draw_recv_list(key, part):
    key = jax.random.fold_in(key, 23)
    return listed_rows(key, N_ROW * N_COL * N_ROW, RCAP)


def draw_tile_count(key, part):
    key = jax.random.fold_in(key, 37)
    first, second, third = jax.random.split(key, 3)
    count_dev = N_ROW * N_COL
    heavy = jax.random.randint(first, (count_dev,), 0, 4) == 0
    light = jax.random.randint(second, (count_dev,), 1, max(TILES // 2, 1) + 1)
    busy = jnp.where(heavy, TILES, light)
    busy = busy.at[0].set(TILES)
    last = jax.random.randint(third, (count_dev,), 1, TILE + 1)
    last = last.at[0].set(TILE)
    index = jnp.arange(TILES, dtype=jnp.int32)[None, :]
    counts = jnp.where(index < busy[:, None] - 1, TILE, jnp.where(index == busy[:, None] - 1, last[:, None], 0))
    return counts.reshape(-1).astype(jnp.int32)


def set_ends(values, own_key, smallest, largest):
    place = [jax.random.randint(jax.random.fold_in(own_key, axis), (), 0, length) for axis, length in enumerate(values.shape)]
    main_axis = values.shape.index(max(values.shape))
    next_to = place[:main_axis] + [(place[main_axis] + 1) % values.shape[main_axis]] + place[main_axis + 1:]
    return values.at[tuple(place)].set(smallest).at[tuple(next_to)].set(largest)


def block_scale(own_key, dims, cuts, low, top_value):
    def one(axis_at, parts):
        steps = jax.random.uniform(jax.random.fold_in(jax.random.fold_in(own_key, 6), axis_at), (parts,), jnp.float32, low / len(cuts), top_value / len(cuts))
        return jnp.repeat(jnp.exp(steps), dims[axis_at] // parts).reshape((-1,) + (1,) * (len(dims) - axis_at - 1))

    factor_of = one(*cuts[0])
    for cut in cuts[1:]:
        factor_of = factor_of * one(*cut)
    return factor_of


def normal_values(key, shape, scale, limit, cuts=(), kind=jnp.bfloat16):
    values = jax.random.normal(key, shape, jnp.float32) * scale
    if len(cuts) > 0:
        values = block_scale(key, shape, cuts, -0.22, 0.18) * values
    return jnp.clip(values, min=-limit, max=limit).astype(kind)


def setup_inputs(seed: int = 0) -> dict:
    splits = jax.random.split(jax.random.key(seed), 18)
    nodes = normal_values(splits[0], (NODES, LATENT), 1.0, 6.0, ((0, 512),))
    edges = normal_values(splits[1], (EDGES, LATENT), 1.0, 6.0, ((0, 512),))
    send_list = draw_send_list(jax.random.fold_in(splits[17], 71), 0)
    recv_list = draw_recv_list(jax.random.fold_in(splits[17], 71), 0)
    sender_slot = set_ends(jax.random.randint(splits[4], (DEVICES * TILES, TILE), 0, N_COL * SCAP), jax.random.fold_in(splits[4], 1), 0, (N_COL * SCAP) - 1).astype(jnp.int32)
    receiver_slot = set_ends(jax.random.randint(splits[5], (DEVICES * TILES, TILE), 0, N_ROW * RCAP), jax.random.fold_in(splits[5], 1), 0, (N_ROW * RCAP) - 1).astype(jnp.int32)
    tile_count = draw_tile_count(jax.random.fold_in(splits[17], 71), 0)
    edge_in_weight = normal_values(splits[7], (3 * LATENT, LATENT), (3 * LATENT) ** -0.5, 0.3125)
    edge_out_weight = normal_values(splits[8], (2, LATENT, LATENT), LATENT ** -0.5, 0.5)
    edge_bias = normal_values(splits[9], (3, LATENT), 0.5, 3.0, (), jnp.float32)
    edge_gain = jnp.clip(1.0 + 0.18 * jax.random.normal(splits[10], (LATENT,), jnp.float32), 0.1, 1.9)
    edge_shift = normal_values(splits[11], (LATENT,), 0.5, 3.0, (), jnp.float32)
    node_in_weight = normal_values(splits[12], (2 * LATENT, LATENT), (2 * LATENT) ** -0.5, 0.375)
    node_out_weight = normal_values(splits[13], (2, LATENT, LATENT), LATENT ** -0.5, 0.5)
    node_bias = normal_values(splits[14], (3, LATENT), 0.5, 3.0, (), jnp.float32)
    node_gain = jnp.clip(1.0 + 0.18 * jax.random.normal(splits[15], (LATENT,), jnp.float32), 0.1, 1.9)
    node_shift = normal_values(splits[16], (LATENT,), 0.5, 3.0, (), jnp.float32)
    return dict(nodes=nodes, edges=edges, send_list=send_list, recv_list=recv_list, sender_slot=sender_slot, receiver_slot=receiver_slot, tile_count=tile_count, edge_in_weight=edge_in_weight, edge_out_weight=edge_out_weight, edge_bias=edge_bias, edge_gain=edge_gain, edge_shift=edge_shift, node_in_weight=node_in_weight, node_out_weight=node_out_weight, node_bias=node_bias, node_gain=node_gain, node_shift=node_shift)


def layer_norm(values, gain, shift):
    mean = lax.optimization_barrier(jnp.mean(values, axis=-1, keepdims=True))
    centred = values - mean
    spread = lax.optimization_barrier(jnp.mean(centred * centred, axis=-1, keepdims=True))
    return centred * lax.rsqrt(spread + 1e-05) * gain + shift

def perceptron(inputs, w_in, w_out, biases, gain, shift):
    hidden = jnp.maximum(jnp.dot(inputs, w_in, preferred_element_type=jnp.float32) + biases[0], 0.0).astype(jnp.bfloat16)
    hidden = jnp.maximum(jnp.dot(hidden, w_out[0], preferred_element_type=jnp.float32) + biases[1], 0.0).astype(jnp.bfloat16)
    output = jnp.dot(hidden, w_out[1], preferred_element_type=jnp.float32) + biases[2]
    return layer_norm(output, gain, shift)

def reference(nodes, edges, send_list, recv_list, sender_slot, receiver_slot, tile_count, edge_in_weight, edge_out_weight, edge_bias, edge_gain, edge_shift, node_in_weight, node_out_weight, node_bias, node_gain, node_shift):
    count_dev = N_ROW * N_COL
    device = jnp.arange(count_dev, dtype=jnp.int32)
    row_of = (device // N_COL)[:, None]
    col_of = (device % N_COL)[:, None]
    sslot = sender_slot.reshape(count_dev, TILES * TILE).astype(jnp.int32)
    rslot = receiver_slot.reshape(count_dev, TILES * TILE).astype(jnp.int32)
    srow = jnp.take_along_axis(send_list.reshape(count_dev, N_COL * SCAP), sslot, axis=1)
    rrow = jnp.take_along_axis(recv_list.reshape(count_dev, N_ROW * RCAP), rslot, axis=1)
    sender = ((row_of * N_COL + sslot // SCAP) * NODE_DEV + srow).reshape(-1).astype(jnp.int32)
    receiver = ((rslot // RCAP * N_COL + col_of) * NODE_DEV + rrow).reshape(-1).astype(jnp.int32)
    counts = tile_count.reshape(count_dev, TILES, 1)
    live = (jnp.arange(TILE, dtype=jnp.int32)[None, None, :] < counts).reshape(-1, 1)
    joined = jnp.concatenate([edges, nodes[sender], nodes[receiver]], axis=1)
    update = perceptron(joined, edge_in_weight, edge_out_weight, edge_bias, edge_gain, edge_shift)
    new_edges = jnp.where(live, edges.astype(jnp.float32) + update, jnp.zeros_like(update)).astype(jnp.bfloat16)
    message = new_edges.astype(jnp.float32)
    total = jnp.zeros((nodes.shape[0], nodes.shape[1]), jnp.float32)
    total = total.at[sender].add(message).at[receiver].add(message)
    joined_nodes = jnp.concatenate([nodes, total.astype(jnp.bfloat16)], axis=1)
    node_update = perceptron(joined_nodes, node_in_weight, node_out_weight, node_bias, node_gain, node_shift)
    new_nodes = (nodes.astype(jnp.float32) + node_update).astype(jnp.bfloat16)
    return (new_nodes, new_edges)
```

```python
import jax
import jax.numpy as jnp
from jax import lax
from jax.experimental import pallas as pl
from jax.experimental.pallas import tpu as pltpu
from jax.sharding import PartitionSpec as P

F32 = jnp.float32
BF16 = jnp.bfloat16
EXTRA = 16
VMEM = pl.BlockSpec(memory_space=pltpu.VMEM)
SMEM = pl.BlockSpec(memory_space=pltpu.SMEM)
NN = (((1,), (0,)), ((), ()))
NT = (((1,), (1,)), ((), ()))
TN = (((0,), (0,)), ((), ()))


def mm(a, b, dims=NN):
    return lax.dot_general(a, b, dims, preferred_element_type=F32)


def repeat_lanes(lists, width):
    depth = lists.shape[1]
    place = (
        lax.broadcasted_iota(jnp.int32, (depth, width), 1) % depth
        == lax.broadcasted_iota(jnp.int32, (depth, width), 0)
    )
    return mm(lists.astype(F32).astype(BF16), place.astype(F32).astype(BF16))


def pack_kernel(nodes_ref, send_list_ref, recv_list_ref, row_ref, col_ref):
    rows, width = nodes_ref.shape
    peers = recv_list_ref.shape[0]
    col_ref[0:rows, :] = nodes_ref[...]
    col_ref[rows : rows + EXTRA, :] = repeat_lanes(send_list_ref[...], width).astype(BF16)
    recv_lanes = repeat_lanes(recv_list_ref[...], width)
    for peer in range(peers):
        row_ref[peer, 0:rows, :] = nodes_ref[...]
        row_ref[peer, rows : rows + EXTRA, :] = jnp.broadcast_to(
            recv_lanes[peer : peer + 1, :], (EXTRA, width)
        ).astype(BF16)


def merge_lists(picked, depth):
    peers, width = picked.shape
    per = width // depth
    lane_block = lax.broadcasted_iota(jnp.int32, (peers, width), 1) // depth
    own = lax.broadcasted_iota(jnp.int32, (peers, width), 0) % per
    kept = jnp.where(lane_block == own, picked, 0.0)
    return [
        jnp.sum(kept[j * per : (j + 1) * per, :], axis=0, keepdims=True)
        for j in range(peers // per)
    ]


def edge_kernel(
    count_ref,
    place_ref,
    row_ref,
    col_ref,
    send_list_ref,
    recv_list_ref,
    send_slot_ref,
    recv_slot_ref,
    edges_ref,
    w_in_ref,
    w_out_ref,
    bias_ref,
    gain_ref,
    shift_ref,
    new_ref,
    send_out_ref,
    recv_out_ref,
    owner_ref,
    send_acc,
    recv_acc,
):
    recv_peers, chunk, width = row_ref.shape
    send_peers = col_ref.shape[0]
    rows = chunk - EXTRA
    send_depth = send_list_ref.shape[1]
    recv_depth = recv_list_ref.shape[1]
    send_width = send_peers * send_depth
    recv_width = recv_peers * recv_depth
    tiles, tile = send_slot_ref.shape
    group = 4
    step_rows = group * tile

    me = place_ref[0]
    mine = lax.broadcasted_iota(jnp.int32, (EXTRA, width), 0) == me
    picked = [
        jnp.sum(
            jnp.where(mine, col_ref[p, rows : rows + EXTRA, :].astype(F32), 0.0),
            axis=0,
            keepdims=True,
        )
        for p in range(send_peers)
    ]
    send_owner = merge_lists(jnp.concatenate(picked, axis=0), send_depth)
    picked = [
        row_ref[p, rows : rows + EXTRA, :].astype(F32)[0:1, :] for p in range(recv_peers)
    ]
    recv_owner = merge_lists(jnp.concatenate(picked, axis=0), recv_depth)
    owner_ref[...] = jnp.concatenate(send_owner + recv_owner, axis=0)

    node_at = lax.broadcasted_iota(jnp.int32, (rows, 1), 0)

    def table(block_ref, list_ref, peers):
        parts = []
        for p in range(peers):
            hot = (node_at == list_ref[p : p + 1, :]).astype(F32).astype(BF16)
            parts.append(mm(hot, block_ref[p, 0:rows, :], TN))
        return jnp.concatenate(parts, axis=0).astype(BF16)

    send_table = table(col_ref, send_list_ref, send_peers)
    recv_table = table(row_ref, recv_list_ref, recv_peers)
    send_proj = mm(send_table, w_in_ref[width : 2 * width, :]).T.astype(BF16)
    recv_proj = mm(recv_table, w_in_ref[2 * width : 3 * width, :]).T.astype(BF16)
    edge_w = w_in_ref[0:width, :].astype(F32).T.astype(BF16)
    mid_w = w_out_ref[0].astype(F32).T.astype(BF16)
    last_w = w_out_ref[1].astype(F32).T.astype(BF16)
    columns = jnp.concatenate(
        [bias_ref[...], gain_ref[...], shift_ref[...], jnp.zeros((3, width), F32)], axis=0
    ).T
    b0, b1, b2 = columns[:, 0:1], columns[:, 1:2], columns[:, 2:3]
    gain, shift = columns[:, 3:4], columns[:, 4:5]

    send_at = lax.broadcasted_iota(jnp.int32, (send_width, tile), 0)
    recv_at = lax.broadcasted_iota(jnp.int32, (recv_width, tile), 0)
    row_at = lax.broadcasted_iota(jnp.int32, (tile, 1), 0)

    for step in range(tiles // group):
        first = step * group
        send_hot = jnp.concatenate(
            [
                (send_at == send_slot_ref[first + t : first + t + 1, :]).astype(F32).astype(BF16)
                for t in range(group)
            ],
            axis=1,
        )
        recv_hot = jnp.concatenate(
            [
                (recv_at == recv_slot_ref[first + t : first + t + 1, :]).astype(F32).astype(BF16)
                for t in range(group)
            ],
            axis=1,
        )
        edge = edges_ref[first * tile : first * tile + step_rows, :]
        hidden = mm(send_proj, send_hot) + mm(recv_proj, recv_hot) + mm(edge_w, edge, NT)
        hidden = jnp.maximum(hidden + b0, 0.0).astype(BF16)
        hidden = jnp.maximum(mm(mid_w, hidden) + b1, 0.0).astype(BF16)
        output = mm(last_w, hidden) + b2
        mean = jnp.sum(output, axis=0, keepdims=True) * (1.0 / width)
        centred = output - mean
        spread = jnp.sum(centred * centred, axis=0, keepdims=True) * (1.0 / width)
        update = (centred * lax.rsqrt(spread + 1e-05) * gain + shift).T
        valid = jnp.concatenate(
            [row_at < count_ref[first + t] for t in range(group)], axis=0
        )
        fresh = jnp.where(valid, edge.astype(F32) + update, 0.0).astype(BF16)
        new_ref[first * tile : first * tile + step_rows, :] = fresh
        send_sum = mm(send_hot, fresh)
        recv_sum = mm(recv_hot, fresh)
        if step == 0:
            send_acc[...] = send_sum
            recv_acc[...] = recv_sum
        else:
            send_acc[...] += send_sum
            recv_acc[...] += recv_sum
    send_out_ref[...] = send_acc[...].astype(BF16).reshape(send_out_ref.shape)
    recv_out_ref[...] = recv_acc[...].astype(BF16).reshape(recv_out_ref.shape)


def node_kernel(
    owner_ref,
    send_ref,
    recv_ref,
    nodes_ref,
    w_in_ref,
    w_out_ref,
    bias_ref,
    gain_ref,
    shift_ref,
    out_ref,
):
    rows, width = nodes_ref.shape
    send = send_ref[...].reshape(-1, width)
    recv = recv_ref[...].reshape(-1, width)
    node_at = lax.broadcasted_iota(jnp.int32, (rows, width), 0).astype(F32)
    send_rows = send.shape[0] // width
    total = jnp.zeros((rows, width), F32)
    for j in range(owner_ref.shape[0]):
        hot = (node_at == owner_ref[j : j + 1, :]).astype(F32).astype(BF16)
        source = send if j < send_rows else recv
        at = (j if j < send_rows else j - send_rows) * width
        total += mm(hot, source[at : at + width, :])
    nodes = nodes_ref[...]
    hidden = mm(nodes, w_in_ref[0:width, :]) + mm(total.astype(BF16), w_in_ref[width : 2 * width, :])
    hidden = jnp.maximum(hidden + bias_ref[0:1, :], 0.0).astype(BF16)
    hidden = jnp.maximum(mm(hidden, w_out_ref[0]) + bias_ref[1:2, :], 0.0).astype(BF16)
    output = mm(hidden, w_out_ref[1]) + bias_ref[2:3, :]
    mean = jnp.mean(output, axis=-1, keepdims=True)
    centred = output - mean
    spread = jnp.mean(centred * centred, axis=-1, keepdims=True)
    update = centred * lax.rsqrt(spread + 1e-05) * gain_ref[...] + shift_ref[...]
    out_ref[...] = (nodes.astype(F32) + update).astype(BF16)


def local(
    nodes,
    edges,
    send_list,
    recv_list,
    sender_slot,
    receiver_slot,
    tile_count,
    edge_in_weight,
    edge_out_weight,
    edge_bias,
    edge_gain,
    edge_shift,
    node_in_weight,
    node_out_weight,
    node_bias,
    node_gain,
    node_shift,
):
    rows, width = nodes.shape
    send_peers, send_depth = send_list.shape
    recv_peers, recv_depth = recv_list.shape
    chunk = rows + EXTRA
    params = pltpu.CompilerParams(vmem_limit_bytes=40 * 1024 * 1024)
    row_send, col_send = pl.pallas_call(
        pack_kernel,
        out_shape=(
            jax.ShapeDtypeStruct((recv_peers, chunk, width), BF16),
            jax.ShapeDtypeStruct((chunk, width), BF16),
        ),
        in_specs=[VMEM] * 3,
        out_specs=(VMEM, VMEM),
        compiler_params=params,
    )(nodes, send_list, recv_list)
    row_block = lax.all_to_all(row_send, "row", 0, 0, tiled=True)
    col_block = lax.all_gather(col_send, "col", axis=0, tiled=True).reshape(
        send_peers, chunk, width
    )
    place = lax.axis_index("col").astype(jnp.int32).reshape(1)
    new_edges, send_part, recv_part, owner = pl.pallas_call(
        edge_kernel,
        out_shape=(
            jax.ShapeDtypeStruct(edges.shape, BF16),
            jax.ShapeDtypeStruct((send_peers, send_depth, width), BF16),
            jax.ShapeDtypeStruct((recv_peers, recv_depth, width), BF16),
            jax.ShapeDtypeStruct((8, width), F32),
        ),
        in_specs=[SMEM, SMEM] + [VMEM] * 12,
        out_specs=(VMEM,) * 4,
        scratch_shapes=[
            pltpu.VMEM((send_peers * send_depth, width), F32),
            pltpu.VMEM((recv_peers * recv_depth, width), F32),
        ],
        compiler_params=params,
        cost_estimate=pl.CostEstimate(
            flops=2 * 10**9, bytes_accessed=4 * 10**6, transcendentals=4096
        ),
    )(
        tile_count,
        place,
        row_block,
        col_block,
        send_list,
        recv_list,
        sender_slot,
        receiver_slot,
        edges,
        edge_in_weight,
        edge_out_weight,
        edge_bias,
        edge_gain.reshape(1, width),
        edge_shift.reshape(1, width),
    )
    recv_in = lax.all_to_all(recv_part, "row", 0, 0, tiled=True)
    send_in = lax.all_to_all(send_part, "col", 0, 0, tiled=True)
    new_nodes = pl.pallas_call(
        node_kernel,
        out_shape=jax.ShapeDtypeStruct(nodes.shape, BF16),
        in_specs=[VMEM] * 9,
        out_specs=VMEM,
        compiler_params=params,
    )(
        owner,
        send_in,
        recv_in,
        nodes,
        node_in_weight,
        node_out_weight,
        node_bias,
        node_gain.reshape(1, width),
        node_shift.reshape(1, width),
    )
    return (new_nodes, new_edges)


def solution(mesh):
    split = P(("row", "col"), None)
    placed = (split,) * 6 + (P(("row", "col")),) + (P(),) * 10
    return jax.shard_map(
        local,
        mesh=mesh,
        in_specs=placed,
        out_specs=(split, split),
        check_vma=False,
    )
```

```python
import jax
import jax.numpy as jnp
from jax import lax
from jax.experimental import pallas as pl
from jax.experimental.pallas import tpu as pltpu
from jax.sharding import PartitionSpec as P

F32 = jnp.float32
BF16 = jnp.bfloat16
I16 = jnp.int16
EXTRA = 16
VMEM = pl.BlockSpec(memory_space=pltpu.VMEM)
SMEM = pl.BlockSpec(memory_space=pltpu.SMEM)
NN = (((1,), (0,)), ((), ()))
NT = (((1,), (1,)), ((), ()))
TN = (((0,), (0,)), ((), ()))


def mm(a, b, dims=NN):
    return lax.dot_general(a, b, dims, preferred_element_type=F32)


def repeat_lanes(lists, width, across):
    depth = lists.shape[across]
    place = (
        lax.broadcasted_iota(jnp.int32, (depth, width), 1) % depth
        == lax.broadcasted_iota(jnp.int32, (depth, width), 0)
    )
    return mm(
        lists.astype(F32).astype(BF16),
        place.astype(F32).astype(BF16),
        (((across,), (0,)), ((), ())),
    )


def pack_kernel(nodes_ref, send_list_ref, recv_list_ref, row_ref, col_ref):
    rows, width = nodes_ref.shape
    peers = recv_list_ref.shape[1]
    col_ref[0:rows, :] = nodes_ref[...]
    col_ref[rows : rows + EXTRA, :] = repeat_lanes(send_list_ref[...], width, 1).astype(BF16)
    recv_lanes = repeat_lanes(recv_list_ref[...], width, 0)
    for peer in range(peers):
        row_ref[peer, 0:rows, :] = nodes_ref[...]
        row_ref[peer, rows : rows + EXTRA, :] = jnp.broadcast_to(
            recv_lanes[peer : peer + 1, :], (EXTRA, width)
        ).astype(BF16)


def merge_lists(picked, depth):
    peers, width = picked.shape
    per = width // depth
    lane_block = lax.broadcasted_iota(jnp.int32, (peers, width), 1) // depth
    own = lax.broadcasted_iota(jnp.int32, (peers, width), 0) % per
    kept = jnp.where(lane_block == own, picked, 0.0)
    return [
        jnp.sum(kept[j * per : (j + 1) * per, :], axis=0, keepdims=True)
        for j in range(peers // per)
    ]


def edge_kernel(
    count_ref,
    place_ref,
    row_ref,
    col_ref,
    send_list_ref,
    recv_list_ref,
    send_slot_ref,
    recv_slot_ref,
    edges_ref,
    w_in_ref,
    w_out_ref,
    bias_ref,
    gain_ref,
    shift_ref,
    new_ref,
    send_out_ref,
    recv_out_ref,
    owner_ref,
):
    recv_peers, chunk, width = row_ref.shape
    send_peers = col_ref.shape[0]
    rows = chunk - EXTRA
    send_depth = send_list_ref.shape[1]
    recv_depth = recv_list_ref.shape[0]
    send_width = send_peers * send_depth
    recv_width = recv_peers * recv_depth
    tiles, tile = send_slot_ref.shape

    me = place_ref[0]
    mine = lax.broadcasted_iota(jnp.int32, (EXTRA, width), 0) == me
    picked = [
        jnp.sum(
            jnp.where(mine, col_ref[p, rows : rows + EXTRA, :].astype(F32), 0.0),
            axis=0,
            keepdims=True,
        )
        for p in range(send_peers)
    ]
    send_owner = merge_lists(jnp.concatenate(picked, axis=0), send_depth)
    picked = [
        row_ref[p, rows : rows + EXTRA, :].astype(F32)[0:1, :] for p in range(recv_peers)
    ]
    recv_owner = merge_lists(jnp.concatenate(picked, axis=0), recv_depth)
    owner_ref[...] = jnp.concatenate(send_owner + recv_owner, axis=0)

    node_at = lax.broadcasted_iota(jnp.int32, (rows, 1), 0)
    node_lane = lax.broadcasted_iota(jnp.int32, (1, rows), 1)
    parts = []
    for p in range(send_peers):
        hot = (node_at == send_list_ref[p : p + 1, :]).astype(F32).astype(BF16)
        parts.append(mm(hot, col_ref[p, 0:rows, :], TN))
    send_table = jnp.concatenate(parts, axis=0).astype(BF16)
    parts = []
    recv_list = recv_list_ref[...]
    for p in range(recv_peers):
        hot = (recv_list[:, p : p + 1] == node_lane).astype(F32).astype(BF16)
        parts.append(mm(hot, row_ref[p, 0:rows, :]))
    recv_table = jnp.concatenate(parts, axis=0).astype(BF16)
    send_proj = mm(send_table, w_in_ref[width : 2 * width, :]).T.astype(BF16)
    recv_proj = mm(recv_table, w_in_ref[2 * width : 3 * width, :]).T.astype(BF16)
    edge_w = w_in_ref[0:width, :].astype(F32).T.astype(BF16)
    mid_w = w_out_ref[0].astype(F32).T.astype(BF16)
    last_w = w_out_ref[1].astype(F32).T.astype(BF16)
    columns = jnp.concatenate(
        [bias_ref[...], gain_ref[...], shift_ref[...], jnp.zeros((3, width), F32)], axis=0
    ).T
    b0, b1, b2 = columns[:, 0:1], columns[:, 1:2], columns[:, 2:3]
    gain, shift = columns[:, 3:4], columns[:, 4:5]

    def one_hot(slot_ref, entries):
        at = lax.broadcasted_iota(jnp.int32, (entries, tile), 0).astype(I16)
        return jnp.concatenate(
            [
                jnp.where(at == slot_ref[t : t + 1, :].astype(I16), BF16(1), BF16(0))
                for t in range(tiles)
            ],
            axis=1,
        )

    send_hot = one_hot(send_slot_ref, send_width)
    recv_hot = one_hot(recv_slot_ref, recv_width)
    edge = edges_ref[...]
    hidden = mm(send_proj, send_hot) + mm(recv_proj, recv_hot) + mm(edge_w, edge, NT)
    hidden = jnp.maximum(hidden + b0, 0.0).astype(BF16)
    hidden = jnp.maximum(mm(mid_w, hidden) + b1, 0.0).astype(BF16)
    output = mm(last_w, hidden) + b2
    mean = jnp.sum(output, axis=0, keepdims=True) * (1.0 / width)
    centred = output - mean
    spread = jnp.sum(centred * centred, axis=0, keepdims=True) * (1.0 / width)
    update = (centred * lax.rsqrt(spread + 1e-05) * gain + shift).T
    row_at = lax.broadcasted_iota(jnp.int32, (tile, 1), 0)
    valid = jnp.concatenate([row_at < count_ref[t] for t in range(tiles)], axis=0)
    fresh = jnp.where(valid, edge.astype(F32) + update, 0.0).astype(BF16)
    new_ref[...] = fresh
    send_out_ref[...] = mm(send_hot, fresh).astype(BF16).reshape(send_out_ref.shape)
    recv_out_ref[...] = mm(recv_hot, fresh).astype(BF16).reshape(recv_out_ref.shape)


def node_kernel(
    owner_ref,
    send_ref,
    recv_ref,
    nodes_ref,
    w_in_ref,
    w_out_ref,
    bias_ref,
    gain_ref,
    shift_ref,
    out_ref,
):
    rows, width = nodes_ref.shape
    send = send_ref[...].reshape(-1, width)
    recv = recv_ref[...].reshape(-1, width)
    node_at = lax.broadcasted_iota(jnp.int32, (rows, width), 0).astype(F32)
    send_rows = send.shape[0] // width
    total = jnp.zeros((rows, width), F32)
    for j in range(owner_ref.shape[0]):
        hot = (node_at == owner_ref[j : j + 1, :]).astype(F32).astype(BF16)
        source = send if j < send_rows else recv
        at = (j if j < send_rows else j - send_rows) * width
        total += mm(hot, source[at : at + width, :])
    nodes = nodes_ref[...]
    hidden = mm(nodes, w_in_ref[0:width, :]) + mm(total.astype(BF16), w_in_ref[width : 2 * width, :])
    hidden = jnp.maximum(hidden + bias_ref[0:1, :], 0.0).astype(BF16)
    hidden = jnp.maximum(mm(hidden, w_out_ref[0]) + bias_ref[1:2, :], 0.0).astype(BF16)
    output = mm(hidden, w_out_ref[1]) + bias_ref[2:3, :]
    mean = jnp.mean(output, axis=-1, keepdims=True)
    centred = output - mean
    spread = jnp.mean(centred * centred, axis=-1, keepdims=True)
    update = centred * lax.rsqrt(spread + 1e-05) * gain_ref[...] + shift_ref[...]
    out_ref[...] = (nodes.astype(F32) + update).astype(BF16)


def local(
    nodes,
    edges,
    send_list,
    recv_list,
    sender_slot,
    receiver_slot,
    tile_count,
    edge_in_weight,
    edge_out_weight,
    edge_bias,
    edge_gain,
    edge_shift,
    node_in_weight,
    node_out_weight,
    node_bias,
    node_gain,
    node_shift,
):
    rows, width = nodes.shape
    send_peers, send_depth = send_list.shape
    recv_list = recv_list.T
    recv_depth, recv_peers = recv_list.shape
    chunk = rows + EXTRA
    params = pltpu.CompilerParams(vmem_limit_bytes=40 * 1024 * 1024)
    row_send, col_send = pl.pallas_call(
        pack_kernel,
        out_shape=(
            jax.ShapeDtypeStruct((recv_peers, chunk, width), BF16),
            jax.ShapeDtypeStruct((chunk, width), BF16),
        ),
        in_specs=[VMEM] * 3,
        out_specs=(VMEM, VMEM),
        compiler_params=pltpu.CompilerParams(vmem_limit_bytes=60 * 1024 * 1024),
    )(nodes, send_list, recv_list)
    row_block = lax.all_to_all(row_send, "row", 0, 0, tiled=True)
    col_block = lax.all_gather(col_send, "col", axis=0, tiled=True).reshape(
        send_peers, chunk, width
    )
    place = lax.axis_index("col").astype(jnp.int32).reshape(1)
    new_edges, send_part, recv_part, owner = pl.pallas_call(
        edge_kernel,
        out_shape=(
            jax.ShapeDtypeStruct(edges.shape, BF16),
            jax.ShapeDtypeStruct((send_peers, send_depth, width), BF16),
            jax.ShapeDtypeStruct((recv_peers, recv_depth, width), BF16),
            jax.ShapeDtypeStruct((8, width), F32),
        ),
        in_specs=[SMEM, SMEM] + [VMEM] * 12,
        out_specs=(VMEM,) * 4,
        compiler_params=params,
        cost_estimate=pl.CostEstimate(
            flops=2 * 10**9, bytes_accessed=4 * 10**6, transcendentals=4096
        ),
    )(
        tile_count,
        place,
        row_block,
        col_block,
        send_list,
        recv_list,
        sender_slot,
        receiver_slot,
        edges,
        edge_in_weight,
        edge_out_weight,
        edge_bias,
        edge_gain.reshape(1, width),
        edge_shift.reshape(1, width),
    )
    recv_in = lax.all_to_all(recv_part, "row", 0, 0, tiled=True)
    send_in = lax.all_to_all(send_part, "col", 0, 0, tiled=True)
    new_nodes = pl.pallas_call(
        node_kernel,
        out_shape=jax.ShapeDtypeStruct(nodes.shape, BF16),
        in_specs=[VMEM] * 9,
        out_specs=VMEM,
        compiler_params=params,
    )(
        owner,
        send_in,
        recv_in,
        nodes,
        node_in_weight,
        node_out_weight,
        node_bias,
        node_gain.reshape(1, width),
        node_shift.reshape(1, width),
    )
    return (new_nodes, new_edges)


def solution(mesh):
    split = P(("row", "col"), None)
    placed = (split,) * 6 + (P(("row", "col")),) + (P(),) * 10
    return jax.shard_map(
        local,
        mesh=mesh,
        in_specs=placed,
        out_specs=(split, split),
        check_vma=False,
    )
```

```python
import jax
import jax.numpy as jnp
from jax import lax
from jax.experimental import pallas as pl
from jax.experimental.pallas import tpu as pltpu
from jax.sharding import PartitionSpec as P

F32 = jnp.float32
BF16 = jnp.bfloat16
I16 = jnp.int16
EXTRA = 16
VMEM = pl.BlockSpec(memory_space=pltpu.VMEM)
SMEM = pl.BlockSpec(memory_space=pltpu.SMEM)
NN = (((1,), (0,)), ((), ()))
NT = (((1,), (1,)), ((), ()))
TN = (((0,), (0,)), ((), ()))


def mm(a, b, dims=NN):
    return lax.dot_general(a, b, dims, preferred_element_type=F32)


def repeat_lanes(lists, width, across):
    depth = lists.shape[across]
    place = (
        lax.broadcasted_iota(jnp.int32, (depth, width), 1) % depth
        == lax.broadcasted_iota(jnp.int32, (depth, width), 0)
    )
    return mm(
        lists.astype(F32).astype(BF16),
        place.astype(F32).astype(BF16),
        (((across,), (0,)), ((), ())),
    )


def pack_kernel(nodes_ref, send_list_ref, recv_list_ref, row_ref, col_ref):
    rows, width = nodes_ref.shape
    peers = recv_list_ref.shape[1]
    col_ref[0:rows, :] = nodes_ref[...]
    col_ref[rows : rows + EXTRA, :] = repeat_lanes(send_list_ref[...], width, 1).astype(BF16)
    recv_lanes = repeat_lanes(recv_list_ref[...], width, 0)
    for peer in range(peers):
        row_ref[peer, 0:rows, :] = nodes_ref[...]
        row_ref[peer, rows : rows + EXTRA, :] = jnp.broadcast_to(
            recv_lanes[peer : peer + 1, :], (EXTRA, width)
        ).astype(BF16)


def merge_lists(picked, depth):
    peers, width = picked.shape
    per = width // depth
    lane_block = lax.broadcasted_iota(jnp.int32, (peers, width), 1) // depth
    own = lax.broadcasted_iota(jnp.int32, (peers, width), 0) % per
    kept = jnp.where(lane_block == own, picked, 0.0)
    return [
        jnp.sum(kept[j * per : (j + 1) * per, :], axis=0, keepdims=True)
        for j in range(peers // per)
    ]


def edge_kernel(
    count_ref,
    place_ref,
    row_ref,
    col_ref,
    send_list_ref,
    recv_list_ref,
    send_slot_ref,
    recv_slot_ref,
    edges_ref,
    w_in_ref,
    w_out_ref,
    bias_ref,
    gain_ref,
    shift_ref,
    new_ref,
    send_out_ref,
    recv_out_ref,
    owner_ref,
    new_vmem,
    sem,
):
    recv_peers, chunk, width = row_ref.shape
    send_peers = col_ref.shape[0]
    rows = chunk - EXTRA
    send_depth = send_list_ref.shape[1]
    recv_depth = recv_list_ref.shape[0]
    send_width = send_peers * send_depth
    recv_width = recv_peers * recv_depth
    tiles, tile = send_slot_ref.shape

    me = place_ref[0]
    mine = lax.broadcasted_iota(jnp.int32, (EXTRA, width), 0) == me
    picked = [
        jnp.sum(
            jnp.where(mine, col_ref[p, rows : rows + EXTRA, :].astype(F32), 0.0),
            axis=0,
            keepdims=True,
        )
        for p in range(send_peers)
    ]
    send_owner = merge_lists(jnp.concatenate(picked, axis=0), send_depth)
    picked = [
        row_ref[p, rows : rows + EXTRA, :].astype(F32)[0:1, :] for p in range(recv_peers)
    ]
    recv_owner = merge_lists(jnp.concatenate(picked, axis=0), recv_depth)
    owner_ref[...] = jnp.concatenate(send_owner + recv_owner, axis=0)

    node_at = lax.broadcasted_iota(jnp.int32, (rows, 1), 0)
    node_lane = lax.broadcasted_iota(jnp.int32, (1, rows), 1)
    parts = []
    for p in range(send_peers):
        hot = (node_at == send_list_ref[p : p + 1, :]).astype(F32).astype(BF16)
        parts.append(mm(hot, col_ref[p, 0:rows, :], TN))
    send_table = jnp.concatenate(parts, axis=0).astype(BF16)
    parts = []
    recv_list = recv_list_ref[...]
    for p in range(recv_peers):
        hot = (recv_list[:, p : p + 1] == node_lane).astype(F32).astype(BF16)
        parts.append(mm(hot, row_ref[p, 0:rows, :]))
    recv_table = jnp.concatenate(parts, axis=0).astype(BF16)
    send_proj = mm(send_table, w_in_ref[width : 2 * width, :]).T.astype(BF16)
    recv_proj = mm(recv_table, w_in_ref[2 * width : 3 * width, :]).T.astype(BF16)
    edge_w = w_in_ref[0:width, :].astype(F32).T.astype(BF16)
    mid_w = w_out_ref[0].astype(F32).T.astype(BF16)
    last_w = w_out_ref[1].astype(F32).T.astype(BF16)
    columns = jnp.concatenate(
        [bias_ref[...], gain_ref[...], shift_ref[...], jnp.zeros((3, width), F32)], axis=0
    ).T
    b0, b1, b2 = columns[:, 0:1], columns[:, 1:2], columns[:, 2:3]
    gain, shift = columns[:, 3:4], columns[:, 4:5]

    def one_hot(slot_ref, entries):
        at = lax.broadcasted_iota(jnp.int32, (entries, tile), 0).astype(I16)
        return jnp.concatenate(
            [
                jnp.where(at == slot_ref[t : t + 1, :].astype(I16), BF16(1), BF16(0))
                for t in range(tiles)
            ],
            axis=1,
        )

    hot = jnp.concatenate(
        [one_hot(send_slot_ref, send_width), one_hot(recv_slot_ref, recv_width)], axis=0
    )
    proj = jnp.concatenate([send_proj, recv_proj], axis=1)
    edge = edges_ref[...]
    hidden = mm(proj, hot) + mm(edge_w, edge, NT)
    hidden = jnp.maximum(hidden + b0, 0.0).astype(BF16)
    hidden = jnp.maximum(mm(mid_w, hidden) + b1, 0.0).astype(BF16)
    output = mm(last_w, hidden) + b2
    mean = jnp.sum(output, axis=0, keepdims=True) * (1.0 / width)
    centred = output - mean
    spread = jnp.sum(centred * centred, axis=0, keepdims=True) * (1.0 / width)
    update = (centred * lax.rsqrt(spread + 1e-05) * gain + shift).T
    row_at = lax.broadcasted_iota(jnp.int32, (tile, 1), 0)
    valid = jnp.concatenate([row_at < count_ref[t] for t in range(tiles)], axis=0)
    fresh = jnp.where(valid, edge.astype(F32) + update, 0.0).astype(BF16)
    new_vmem[...] = fresh
    copy = pltpu.make_async_copy(new_vmem, new_ref, sem)
    copy.start()
    sums = mm(hot, fresh).astype(BF16)
    send_out_ref[...] = sums[0:send_width, :].reshape(send_out_ref.shape)
    recv_out_ref[...] = sums[send_width:, :].reshape(recv_out_ref.shape)
    copy.wait()


def node_kernel(
    owner_ref,
    send_ref,
    recv_ref,
    nodes_ref,
    w_in_ref,
    w_out_ref,
    bias_ref,
    gain_ref,
    shift_ref,
    out_ref,
):
    rows, width = nodes_ref.shape
    partial = jnp.concatenate(
        [send_ref[...].reshape(-1, width), recv_ref[...].reshape(-1, width)], axis=0
    )
    node_at = lax.broadcasted_iota(jnp.int32, (rows, width), 0).astype(F32)
    hot = jnp.concatenate(
        [
            (node_at == owner_ref[j : j + 1, :]).astype(F32).astype(BF16)
            for j in range(owner_ref.shape[0])
        ],
        axis=1,
    )
    total = mm(hot, partial)
    nodes = nodes_ref[...]
    hidden = mm(nodes, w_in_ref[0:width, :]) + mm(total.astype(BF16), w_in_ref[width : 2 * width, :])
    hidden = jnp.maximum(hidden + bias_ref[0:1, :], 0.0).astype(BF16)
    hidden = jnp.maximum(mm(hidden, w_out_ref[0]) + bias_ref[1:2, :], 0.0).astype(BF16)
    output = mm(hidden, w_out_ref[1]) + bias_ref[2:3, :]
    mean = jnp.mean(output, axis=-1, keepdims=True)
    centred = output - mean
    spread = jnp.mean(centred * centred, axis=-1, keepdims=True)
    update = centred * lax.rsqrt(spread + 1e-05) * gain_ref[...] + shift_ref[...]
    out_ref[...] = (nodes.astype(F32) + update).astype(BF16)


def local(
    nodes,
    edges,
    send_list,
    recv_list,
    sender_slot,
    receiver_slot,
    tile_count,
    edge_in_weight,
    edge_out_weight,
    edge_bias,
    edge_gain,
    edge_shift,
    node_in_weight,
    node_out_weight,
    node_bias,
    node_gain,
    node_shift,
):
    rows, width = nodes.shape
    send_peers, send_depth = send_list.shape
    recv_list = recv_list.T
    recv_depth, recv_peers = recv_list.shape
    chunk = rows + EXTRA
    params = pltpu.CompilerParams(vmem_limit_bytes=40 * 1024 * 1024)
    row_send, col_send = pl.pallas_call(
        pack_kernel,
        out_shape=(
            jax.ShapeDtypeStruct((recv_peers, chunk, width), BF16),
            jax.ShapeDtypeStruct((chunk, width), BF16),
        ),
        in_specs=[VMEM] * 3,
        out_specs=(VMEM, VMEM),
        compiler_params=pltpu.CompilerParams(vmem_limit_bytes=60 * 1024 * 1024),
    )(nodes, send_list, recv_list)
    row_block = lax.all_to_all(row_send, "row", 0, 0, tiled=True)
    col_block = lax.all_gather(col_send, "col", axis=0, tiled=True).reshape(
        send_peers, chunk, width
    )
    place = lax.axis_index("col").astype(jnp.int32).reshape(1)
    new_edges, send_part, recv_part, owner = pl.pallas_call(
        edge_kernel,
        out_shape=(
            jax.ShapeDtypeStruct(edges.shape, BF16),
            jax.ShapeDtypeStruct((send_peers, send_depth, width), BF16),
            jax.ShapeDtypeStruct((recv_peers, recv_depth, width), BF16),
            jax.ShapeDtypeStruct((8, width), F32),
        ),
        in_specs=[SMEM, SMEM] + [VMEM] * 12,
        out_specs=(pl.BlockSpec(memory_space=pl.ANY), VMEM, VMEM, VMEM),
        scratch_shapes=[pltpu.VMEM(edges.shape, BF16), pltpu.SemaphoreType.DMA(())],
        compiler_params=params,
        cost_estimate=pl.CostEstimate(
            flops=2 * 10**9, bytes_accessed=4 * 10**6, transcendentals=4096
        ),
    )(
        tile_count,
        place,
        row_block,
        col_block,
        send_list,
        recv_list,
        sender_slot,
        receiver_slot,
        edges,
        edge_in_weight,
        edge_out_weight,
        edge_bias,
        edge_gain.reshape(1, width),
        edge_shift.reshape(1, width),
    )
    recv_in = lax.all_to_all(recv_part, "row", 0, 0, tiled=True)
    send_in = lax.all_to_all(send_part, "col", 0, 0, tiled=True)
    new_nodes = pl.pallas_call(
        node_kernel,
        out_shape=jax.ShapeDtypeStruct(nodes.shape, BF16),
        in_specs=[VMEM] * 9,
        out_specs=VMEM,
        compiler_params=params,
    )(
        owner,
        send_in,
        recv_in,
        nodes,
        node_in_weight,
        node_out_weight,
        node_bias,
        node_gain.reshape(1, width),
        node_shift.reshape(1, width),
    )
    return (new_nodes, new_edges)


def solution(mesh):
    split = P(("row", "col"), None)
    placed = (split,) * 6 + (P(("row", "col")),) + (P(),) * 10
    return jax.shard_map(
        local,
        mesh=mesh,
        in_specs=placed,
        out_specs=(split, split),
        check_vma=False,
    )
```

```python
import jax
import jax.numpy as jnp
from jax import lax
from jax.experimental import pallas as pl
from jax.experimental.pallas import tpu as pltpu
from jax.sharding import PartitionSpec as P

F32 = jnp.float32
BF16 = jnp.bfloat16
I16 = jnp.int16
EXTRA = 16
VMEM = pl.BlockSpec(memory_space=pltpu.VMEM)
SMEM = pl.BlockSpec(memory_space=pltpu.SMEM)
NN = (((1,), (0,)), ((), ()))
NT = (((1,), (1,)), ((), ()))
TN = (((0,), (0,)), ((), ()))


def mm(a, b, dims=NN):
    return lax.dot_general(a, b, dims, preferred_element_type=F32)


def repeat_lanes(lists, width, across):
    depth = lists.shape[across]
    place = (
        lax.broadcasted_iota(jnp.int32, (depth, width), 1) % depth
        == lax.broadcasted_iota(jnp.int32, (depth, width), 0)
    )
    return mm(
        lists.astype(F32).astype(BF16),
        place.astype(F32).astype(BF16),
        (((across,), (0,)), ((), ())),
    )


def pack_kernel(nodes_ref, send_list_ref, recv_list_ref, row_ref, col_ref):
    rows, width = nodes_ref.shape
    peers = recv_list_ref.shape[1]
    col_ref[0:rows, :] = nodes_ref[...]
    col_ref[rows : rows + EXTRA, :] = repeat_lanes(send_list_ref[...], width, 1).astype(BF16)
    recv_lanes = repeat_lanes(recv_list_ref[...], width, 0)
    for peer in range(peers):
        row_ref[peer, 0:rows, :] = nodes_ref[...]
        row_ref[peer, rows : rows + EXTRA, :] = jnp.broadcast_to(
            recv_lanes[peer : peer + 1, :], (EXTRA, width)
        ).astype(BF16)


def merge_lists(picked, depth):
    peers, width = picked.shape
    per = width // depth
    lane_block = lax.broadcasted_iota(jnp.int32, (peers, width), 1) // depth
    own = lax.broadcasted_iota(jnp.int32, (peers, width), 0) % per
    kept = jnp.where(lane_block == own, picked, 0.0)
    return [
        jnp.sum(kept[j * per : (j + 1) * per, :], axis=0, keepdims=True)
        for j in range(peers // per)
    ]


def edge_kernel(
    count_ref,
    place_ref,
    row_ref,
    col_ref,
    send_list_ref,
    recv_list_ref,
    send_slot_ref,
    recv_slot_ref,
    edges_ref,
    w_in_ref,
    w_out_ref,
    bias_ref,
    gain_ref,
    shift_ref,
    new_ref,
    send_out_ref,
    recv_out_ref,
    owner_ref,
    new_vmem,
    sem,
):
    recv_peers, chunk, width = row_ref.shape
    send_peers = col_ref.shape[0]
    rows = chunk - EXTRA
    send_depth = send_list_ref.shape[1]
    recv_depth = recv_list_ref.shape[0]
    send_width = send_peers * send_depth
    recv_width = recv_peers * recv_depth
    tiles, tile = send_slot_ref.shape

    me = place_ref[0]
    mine = lax.broadcasted_iota(jnp.int32, (EXTRA, width), 0) == me
    picked = [
        jnp.sum(
            jnp.where(mine, col_ref[p, rows : rows + EXTRA, :].astype(F32), 0.0),
            axis=0,
            keepdims=True,
        )
        for p in range(send_peers)
    ]
    send_owner = merge_lists(jnp.concatenate(picked, axis=0), send_depth)
    picked = [
        row_ref[p, rows : rows + EXTRA, :].astype(F32)[0:1, :] for p in range(recv_peers)
    ]
    recv_owner = merge_lists(jnp.concatenate(picked, axis=0), recv_depth)
    owner_ref[...] = jnp.concatenate(send_owner + recv_owner, axis=0)

    node_at = lax.broadcasted_iota(jnp.int32, (rows, 1), 0)
    node_lane = lax.broadcasted_iota(jnp.int32, (1, rows), 1)
    parts = []
    for p in range(send_peers):
        hot = (node_at == send_list_ref[p : p + 1, :]).astype(F32).astype(BF16)
        parts.append(mm(hot, col_ref[p, 0:rows, :], TN))
    send_table = jnp.concatenate(parts, axis=0).astype(BF16)
    parts = []
    recv_list = recv_list_ref[...]
    for p in range(recv_peers):
        hot = (recv_list[:, p : p + 1] == node_lane).astype(F32).astype(BF16)
        parts.append(mm(hot, row_ref[p, 0:rows, :]))
    recv_table = jnp.concatenate(parts, axis=0).astype(BF16)
    send_proj = mm(send_table, w_in_ref[width : 2 * width, :]).T.astype(BF16)
    recv_proj = mm(recv_table, w_in_ref[2 * width : 3 * width, :]).T.astype(BF16)
    edge_w = w_in_ref[0:width, :].astype(F32).T.astype(BF16)
    mid_w = w_out_ref[0].astype(F32).T.astype(BF16)
    last_w = w_out_ref[1].astype(F32).T.astype(BF16)
    columns = jnp.concatenate(
        [bias_ref[...], gain_ref[...], shift_ref[...], jnp.zeros((3, width), F32)], axis=0
    ).T
    b0, b1, b2 = columns[:, 0:1], columns[:, 1:2], columns[:, 2:3]
    gain, shift = columns[:, 3:4], columns[:, 4:5]

    def one_hot(slot_ref, entries):
        at = lax.broadcasted_iota(jnp.int32, (entries, tile), 0).astype(I16)
        return jnp.concatenate(
            [
                jnp.where(at == slot_ref[t : t + 1, :].astype(I16), BF16(1), BF16(0))
                for t in range(tiles)
            ],
            axis=1,
        )

    hot = jnp.concatenate(
        [one_hot(send_slot_ref, send_width), one_hot(recv_slot_ref, recv_width)], axis=0
    )
    proj = jnp.concatenate([send_proj, recv_proj], axis=1)
    edge = edges_ref[...]
    hidden = mm(proj, hot) + mm(edge_w, edge, NT)
    hidden = jnp.maximum(hidden + b0, 0.0).astype(BF16)
    hidden = jnp.maximum(mm(mid_w, hidden) + b1, 0.0).astype(BF16)
    output = mm(last_w, hidden) + b2
    mean = jnp.sum(output, axis=0, keepdims=True) * (1.0 / width)
    centred = output - mean
    spread = jnp.sum(centred * centred, axis=0, keepdims=True) * (1.0 / width)
    update = (centred * lax.rsqrt(spread + 1e-05) * gain + shift).T
    row_at = lax.broadcasted_iota(jnp.int32, (tile, 1), 0)
    valid = jnp.concatenate([row_at < count_ref[t] for t in range(tiles)], axis=0)
    fresh = jnp.where(valid, edge.astype(F32) + update, 0.0).astype(BF16)
    new_vmem[...] = fresh
    copy = pltpu.make_async_copy(new_vmem, new_ref, sem)
    copy.start()
    sums = mm(hot, fresh).astype(BF16)
    send_out_ref[...] = sums[0:send_width, :].reshape(send_out_ref.shape)
    recv_out_ref[...] = sums[send_width:, :].reshape(recv_out_ref.shape)
    copy.wait()


def node_kernel(
    owner_ref,
    send_ref,
    recv_ref,
    nodes_ref,
    w_in_ref,
    w_out_ref,
    bias_ref,
    gain_ref,
    shift_ref,
    out_ref,
):
    rows, width = nodes_ref.shape
    partial = jnp.concatenate(
        [send_ref[...].reshape(-1, width), recv_ref[...].reshape(-1, width)], axis=0
    )
    node_at = lax.broadcasted_iota(jnp.int32, (rows, width), 0).astype(F32)
    hot = jnp.concatenate(
        [
            (node_at == owner_ref[j : j + 1, :]).astype(F32).astype(BF16)
            for j in range(owner_ref.shape[0])
        ],
        axis=1,
    )
    total = mm(hot, partial)
    nodes = nodes_ref[...]
    hidden = mm(nodes, w_in_ref[0:width, :]) + mm(total.astype(BF16), w_in_ref[width : 2 * width, :])
    hidden = jnp.maximum(hidden + bias_ref[0:1, :], 0.0).astype(BF16)
    hidden = jnp.maximum(mm(hidden, w_out_ref[0]) + bias_ref[1:2, :], 0.0).astype(BF16)
    output = mm(hidden, w_out_ref[1]) + bias_ref[2:3, :]
    mean = jnp.mean(output, axis=-1, keepdims=True)
    centred = output - mean
    spread = jnp.mean(centred * centred, axis=-1, keepdims=True)
    update = centred * lax.rsqrt(spread + 1e-05) * gain_ref[...] + shift_ref[...]
    out_ref[...] = (nodes.astype(F32) + update).astype(BF16)


def local(
    nodes,
    edges,
    send_list,
    recv_list,
    sender_slot,
    receiver_slot,
    tile_count,
    edge_in_weight,
    edge_out_weight,
    edge_bias,
    edge_gain,
    edge_shift,
    node_in_weight,
    node_out_weight,
    node_bias,
    node_gain,
    node_shift,
):
    rows, width = nodes.shape
    send_peers, send_depth = send_list.shape
    recv_list = recv_list.T
    recv_depth, recv_peers = recv_list.shape
    chunk = rows + EXTRA
    params = pltpu.CompilerParams(vmem_limit_bytes=40 * 1024 * 1024)
    row_send, col_send = pl.pallas_call(
        pack_kernel,
        out_shape=(
            jax.ShapeDtypeStruct((recv_peers, chunk, width), BF16),
            jax.ShapeDtypeStruct((chunk, width), BF16),
        ),
        in_specs=[VMEM] * 3,
        out_specs=(VMEM, VMEM),
        compiler_params=pltpu.CompilerParams(vmem_limit_bytes=60 * 1024 * 1024),
    )(nodes, send_list, recv_list)
    row_block = lax.all_to_all(row_send, "row", 0, 0, tiled=True)
    col_block = lax.all_gather(col_send, "col", axis=0, tiled=True).reshape(
        send_peers, chunk, width
    )
    place = lax.axis_index("col").astype(jnp.int32).reshape(1)
    new_edges, send_part, recv_part, owner = pl.pallas_call(
        edge_kernel,
        out_shape=(
            jax.ShapeDtypeStruct(edges.shape, BF16),
            jax.ShapeDtypeStruct((send_peers, send_depth, width), BF16),
            jax.ShapeDtypeStruct((recv_peers, recv_depth, width), BF16),
            jax.ShapeDtypeStruct((8, width), F32),
        ),
        in_specs=[SMEM, SMEM] + [VMEM] * 12,
        out_specs=(pl.BlockSpec(memory_space=pl.ANY), VMEM, VMEM, VMEM),
        scratch_shapes=[pltpu.VMEM(edges.shape, BF16), pltpu.SemaphoreType.DMA(())],
        compiler_params=params,
        cost_estimate=pl.CostEstimate(
            flops=2 * 10**9, bytes_accessed=4 * 10**6, transcendentals=4096
        ),
    )(
        tile_count,
        place,
        row_block,
        col_block,
        send_list,
        recv_list,
        sender_slot,
        receiver_slot,
        edges,
        edge_in_weight,
        edge_out_weight,
        edge_bias,
        edge_gain.reshape(1, width),
        edge_shift.reshape(1, width),
    )
    send_in = lax.all_to_all(send_part, "col", 0, 0, tiled=True)
    send_in, recv_part = lax.optimization_barrier((send_in, recv_part))
    recv_in = lax.all_to_all(recv_part, "row", 0, 0, tiled=True)
    new_nodes = pl.pallas_call(
        node_kernel,
        out_shape=jax.ShapeDtypeStruct(nodes.shape, BF16),
        in_specs=[VMEM] * 9,
        out_specs=VMEM,
        compiler_params=params,
    )(
        owner,
        send_in,
        recv_in,
        nodes,
        node_in_weight,
        node_out_weight,
        node_bias,
        node_gain.reshape(1, width),
        node_shift.reshape(1, width),
    )
    return (new_nodes, new_edges)


def solution(mesh):
    split = P(("row", "col"), None)
    placed = (split,) * 6 + (P(("row", "col")),) + (P(),) * 10
    return jax.shard_map(
        local,
        mesh=mesh,
        in_specs=placed,
        out_specs=(split, split),
        check_vma=False,
    )
```

```python
import jax
import jax.numpy as jnp
from jax import lax
from jax.experimental import pallas as pl
from jax.experimental.pallas import tpu as pltpu
from jax.sharding import PartitionSpec as P

F32 = jnp.float32
BF16 = jnp.bfloat16
I16 = jnp.int16
EXTRA = 16
VMEM = pl.BlockSpec(memory_space=pltpu.VMEM)
SMEM = pl.BlockSpec(memory_space=pltpu.SMEM)
NN = (((1,), (0,)), ((), ()))
NT = (((1,), (1,)), ((), ()))
TN = (((0,), (0,)), ((), ()))


def mm(a, b, dims=NN):
    return lax.dot_general(a, b, dims, preferred_element_type=F32)


def repeat_lanes(lists, width, across):
    depth = lists.shape[across]
    place = (
        lax.broadcasted_iota(jnp.int32, (depth, width), 1) % depth
        == lax.broadcasted_iota(jnp.int32, (depth, width), 0)
    )
    return mm(
        lists.astype(F32).astype(BF16),
        place.astype(F32).astype(BF16),
        (((across,), (0,)), ((), ())),
    )


def pack_kernel(nodes_ref, send_list_ref, recv_list_ref, row_ref, col_ref):
    rows, width = nodes_ref.shape
    peers = recv_list_ref.shape[1]
    col_ref[0:rows, :] = nodes_ref[...]
    col_ref[rows : rows + EXTRA, :] = repeat_lanes(send_list_ref[...], width, 1).astype(BF16)
    recv_lanes = repeat_lanes(recv_list_ref[...], width, 0)
    for peer in range(peers):
        row_ref[peer, 0:rows, :] = nodes_ref[...]
        row_ref[peer, rows : rows + EXTRA, :] = jnp.broadcast_to(
            recv_lanes[peer : peer + 1, :], (EXTRA, width)
        ).astype(BF16)


def merge_lists(picked, depth):
    peers, width = picked.shape
    per = width // depth
    lane_block = lax.broadcasted_iota(jnp.int32, (peers, width), 1) // depth
    own = lax.broadcasted_iota(jnp.int32, (peers, width), 0) % per
    kept = jnp.where(lane_block == own, picked, 0.0)
    return [
        jnp.sum(kept[j * per : (j + 1) * per, :], axis=0, keepdims=True)
        for j in range(peers // per)
    ]


def edge_kernel(
    count_ref,
    place_ref,
    row_ref,
    col_ref,
    send_list_ref,
    recv_list_ref,
    send_slot_ref,
    recv_slot_ref,
    edges_ref,
    w_in_ref,
    w_out_ref,
    bias_ref,
    gain_ref,
    shift_ref,
    new_ref,
    send_out_ref,
    recv_out_ref,
    owner_ref,
    new_vmem,
    sem,
):
    recv_peers, chunk, width = row_ref.shape
    send_peers = col_ref.shape[0]
    rows = chunk - EXTRA
    send_depth = send_list_ref.shape[1]
    recv_depth = recv_list_ref.shape[0]
    send_width = send_peers * send_depth
    recv_width = recv_peers * recv_depth
    tiles, tile = send_slot_ref.shape

    me = place_ref[0]
    mine = lax.broadcasted_iota(jnp.int32, (EXTRA, width), 0) == me
    picked = [
        jnp.sum(
            jnp.where(mine, col_ref[p, rows : rows + EXTRA, :].astype(F32), 0.0),
            axis=0,
            keepdims=True,
        )
        for p in range(send_peers)
    ]
    send_owner = merge_lists(jnp.concatenate(picked, axis=0), send_depth)
    picked = [
        row_ref[p, rows : rows + EXTRA, :].astype(F32)[0:1, :] for p in range(recv_peers)
    ]
    recv_owner = merge_lists(jnp.concatenate(picked, axis=0), recv_depth)
    owner_ref[...] = jnp.concatenate(send_owner + recv_owner, axis=0)

    node_at = lax.broadcasted_iota(jnp.int32, (rows, 1), 0)
    node_lane = lax.broadcasted_iota(jnp.int32, (1, rows), 1)
    parts = []
    for p in range(send_peers):
        hot = (node_at == send_list_ref[p : p + 1, :]).astype(F32).astype(BF16)
        parts.append(mm(hot, col_ref[p, 0:rows, :], TN))
    send_table = jnp.concatenate(parts, axis=0).astype(BF16)
    parts = []
    recv_list = recv_list_ref[...]
    for p in range(recv_peers):
        hot = (recv_list[:, p : p + 1] == node_lane).astype(F32).astype(BF16)
        parts.append(mm(hot, row_ref[p, 0:rows, :]))
    recv_table = jnp.concatenate(parts, axis=0).astype(BF16)
    send_proj = mm(send_table, w_in_ref[width : 2 * width, :]).T.astype(BF16)
    recv_proj = mm(recv_table, w_in_ref[2 * width : 3 * width, :]).T.astype(BF16)
    edge_w = w_in_ref[0:width, :].astype(F32).T.astype(BF16)
    mid_w = w_out_ref[0].astype(F32).T.astype(BF16)
    last_w = w_out_ref[1].astype(F32).T.astype(BF16)
    columns = jnp.concatenate(
        [bias_ref[...], gain_ref[...], shift_ref[...], jnp.zeros((3, width), F32)], axis=0
    ).T
    b0, b1, b2 = columns[:, 0:1], columns[:, 1:2], columns[:, 2:3]
    gain, shift = columns[:, 3:4], columns[:, 4:5]

    def one_hot(slot_ref, entries):
        at = lax.broadcasted_iota(jnp.int32, (entries, tile), 0).astype(I16)
        return jnp.concatenate(
            [
                jnp.where(at == slot_ref[t : t + 1, :].astype(I16), BF16(1), BF16(0))
                for t in range(tiles)
            ],
            axis=1,
        )

    hot = jnp.concatenate(
        [one_hot(send_slot_ref, send_width), one_hot(recv_slot_ref, recv_width)], axis=0
    )
    proj = jnp.concatenate([send_proj, recv_proj], axis=1)
    edge = edges_ref[...]
    hidden = mm(proj, hot) + mm(edge_w, edge, NT)
    hidden = jnp.maximum((hidden + b0).astype(BF16), BF16(0))
    hidden = jnp.maximum((mm(mid_w, hidden) + b1).astype(BF16), BF16(0))
    output = mm(last_w, hidden) + b2
    mean = jnp.sum(output, axis=0, keepdims=True) * (1.0 / width)
    centred = output - mean
    spread = jnp.sum(centred * centred, axis=0, keepdims=True) * (1.0 / width)
    update = (centred * lax.rsqrt(spread + 1e-05) * gain + shift).T
    row_at = lax.broadcasted_iota(jnp.int32, (tile, 1), 0)
    valid = jnp.concatenate([row_at < count_ref[t] for t in range(tiles)], axis=0)
    fresh = jnp.where(valid, edge.astype(F32) + update, 0.0).astype(BF16)
    new_vmem[...] = fresh
    copy = pltpu.make_async_copy(new_vmem, new_ref, sem)
    copy.start()
    sums = mm(hot, fresh).astype(BF16)
    send_out_ref[...] = sums[0:send_width, :].reshape(send_out_ref.shape)
    recv_out_ref[...] = sums[send_width:, :].reshape(recv_out_ref.shape)
    copy.wait()


def node_kernel(
    owner_ref,
    send_ref,
    recv_ref,
    nodes_ref,
    w_in_ref,
    w_out_ref,
    bias_ref,
    gain_ref,
    shift_ref,
    out_ref,
):
    rows, width = nodes_ref.shape
    partial = jnp.concatenate(
        [send_ref[...].reshape(-1, width), recv_ref[...].reshape(-1, width)], axis=0
    )
    node_at = lax.broadcasted_iota(jnp.int32, (rows, width), 0).astype(F32)
    hot = jnp.concatenate(
        [
            (node_at == owner_ref[j : j + 1, :]).astype(F32).astype(BF16)
            for j in range(owner_ref.shape[0])
        ],
        axis=1,
    )
    total = mm(hot, partial)
    nodes = nodes_ref[...]
    hidden = mm(nodes, w_in_ref[0:width, :]) + mm(total.astype(BF16), w_in_ref[width : 2 * width, :])
    hidden = jnp.maximum(hidden + bias_ref[0:1, :], 0.0).astype(BF16)
    hidden = jnp.maximum(mm(hidden, w_out_ref[0]) + bias_ref[1:2, :], 0.0).astype(BF16)
    output = mm(hidden, w_out_ref[1]) + bias_ref[2:3, :]
    mean = jnp.mean(output, axis=-1, keepdims=True)
    centred = output - mean
    spread = jnp.mean(centred * centred, axis=-1, keepdims=True)
    update = centred * lax.rsqrt(spread + 1e-05) * gain_ref[...] + shift_ref[...]
    out_ref[...] = (nodes.astype(F32) + update).astype(BF16)


def local(
    nodes,
    edges,
    send_list,
    recv_list,
    sender_slot,
    receiver_slot,
    tile_count,
    edge_in_weight,
    edge_out_weight,
    edge_bias,
    edge_gain,
    edge_shift,
    node_in_weight,
    node_out_weight,
    node_bias,
    node_gain,
    node_shift,
):
    rows, width = nodes.shape
    send_peers, send_depth = send_list.shape
    recv_list = recv_list.T
    recv_depth, recv_peers = recv_list.shape
    chunk = rows + EXTRA
    params = pltpu.CompilerParams(vmem_limit_bytes=40 * 1024 * 1024)
    row_send, col_send = pl.pallas_call(
        pack_kernel,
        out_shape=(
            jax.ShapeDtypeStruct((recv_peers, chunk, width), BF16),
            jax.ShapeDtypeStruct((chunk, width), BF16),
        ),
        in_specs=[VMEM] * 3,
        out_specs=(VMEM, VMEM),
        compiler_params=pltpu.CompilerParams(vmem_limit_bytes=60 * 1024 * 1024),
    )(nodes, send_list, recv_list)
    row_block = lax.all_to_all(row_send, "row", 0, 0, tiled=True)
    col_block = lax.all_gather(col_send, "col", axis=0, tiled=True).reshape(
        send_peers, chunk, width
    )
    place = lax.axis_index("col").astype(jnp.int32).reshape(1)
    new_edges, send_part, recv_part, owner = pl.pallas_call(
        edge_kernel,
        out_shape=(
            jax.ShapeDtypeStruct(edges.shape, BF16),
            jax.ShapeDtypeStruct((send_peers, send_depth, width), BF16),
            jax.ShapeDtypeStruct((recv_peers, recv_depth, width), BF16),
            jax.ShapeDtypeStruct((8, width), F32),
        ),
        in_specs=[SMEM, SMEM] + [VMEM] * 12,
        out_specs=(pl.BlockSpec(memory_space=pl.ANY), VMEM, VMEM, VMEM),
        scratch_shapes=[pltpu.VMEM(edges.shape, BF16), pltpu.SemaphoreType.DMA(())],
        compiler_params=params,
        cost_estimate=pl.CostEstimate(
            flops=2 * 10**9, bytes_accessed=4 * 10**6, transcendentals=4096
        ),
    )(
        tile_count,
        place,
        row_block,
        col_block,
        send_list,
        recv_list,
        sender_slot,
        receiver_slot,
        edges,
        edge_in_weight,
        edge_out_weight,
        edge_bias,
        edge_gain.reshape(1, width),
        edge_shift.reshape(1, width),
    )
    recv_in = lax.all_to_all(recv_part, "row", 0, 0, tiled=True)
    send_in = lax.all_to_all(send_part, "col", 0, 0, tiled=True)
    new_nodes = pl.pallas_call(
        node_kernel,
        out_shape=jax.ShapeDtypeStruct(nodes.shape, BF16),
        in_specs=[VMEM] * 9,
        out_specs=VMEM,
        compiler_params=params,
    )(
        owner,
        send_in,
        recv_in,
        nodes,
        node_in_weight,
        node_out_weight,
        node_bias,
        node_gain.reshape(1, width),
        node_shift.reshape(1, width),
    )
    return (new_nodes, new_edges)


def solution(mesh):
    split = P(("row", "col"), None)
    placed = (split,) * 6 + (P(("row", "col")),) + (P(),) * 10
    return jax.shard_map(
        local,
        mesh=mesh,
        in_specs=placed,
        out_specs=(split, split),
        check_vma=False,
    )
```
